512 devices in a mesh: row: 32 (over y, x, z_hi), col: 16 (over z_lo, core).
Axes of the slice: x: 4, y: 4, z: 16 (z_hi: 2, z_lo: 8; z = z_hi * 8 + z_lo), core: 2. Of those that a mesh axis runs over, the one named last changes fastest.
Arguments:
- grads: bfloat16 [4096, 8192], P(('row', 'col')), as said below
Outputs:
- gram: float32 [4096, 4096], P('row', 'col')
Inputs may be any that keep to these rules, and one draw needn't show every extreme that they name: `grads`: each row is a real-valued projected gradient.
All inputs are finite; a program needn't handle non-finite values.
Results may differ from the reference program's by a relative error of at most 0.0003.
Values may be sent and summed in bfloat16 or wider, within the bound.
No kernel may reach another device: no remote copies, remote signals or barrier semaphores. Data moves between devices by JAX's collectives and lax.ppermute only.
A program may use at most 64 MiB of HBM per device.

```python
import jax
import jax.numpy as jnp
from jax import lax

K = 8192
EXAMPLES = 4096
FACTORS = 16


def draw_grads(key, part):
    key = jax.random.fold_in(key, 7)
    keys = jax.random.split(key, 6)
    basis = jax.random.normal(keys[0], (FACTORS, K), jnp.float32)
    ranks = jnp.arange(FACTORS).astype(jnp.float32)
    spread = 0.8 / jnp.sqrt(ranks + 1.0)
    coeffs = jax.random.normal(keys[1], (EXAMPLES, FACTORS), jnp.float32) * spread[None, :]
    members = jax.random.permutation(keys[4], EXAMPLES) // 4
    shared = jax.random.normal(keys[5], ((EXAMPLES + 3) // 4, K), jnp.float32)
    noise = jax.random.normal(keys[2], (EXAMPLES, K), jnp.float32)
    scales = jnp.exp(jax.random.uniform(keys[3], (EXAMPLES, 1), jnp.float32, -1.2, 1.2))
    total = noise + 0.9 * jnp.take(shared, members, axis=0)
    for index in range(FACTORS):
        total = total + coeffs[:, index:index + 1] * basis[index][None, :]
    return (total * scales).astype(jnp.bfloat16)


def setup_inputs(seed: int = 0) -> dict:
    arg_keys = jax.random.split(jax.random.key(seed), 2)
    grads = draw_grads(jax.random.fold_in(arg_keys[1], 71), 0)
    return {"grads": grads}


def reference(grads):
    wide = grads.astype(jnp.float32)
    inverse = lax.rsqrt(lax.optimization_barrier(jnp.sum(wide * wide, axis=1)) + 1e-06)
    products = lax.dot_general(grads, grads, (((1,), (1,)), ((), ())), preferred_element_type=jnp.float32)
    return inverse[:, None] * products * inverse[None, :]
```

```python
import jax
import jax.numpy as jnp
from jax import lax
from jax.sharding import Mesh, PartitionSpec as P

AXES = ("y", "x", "zh", "zl", "core")
SIZES = (4, 4, 2, 8, 2)
Z = ("zh", "zl")


def inverse_norms(block):
    wide = block.astype(jnp.float32)
    return lax.rsqrt(jnp.sum(wide * wide, axis=1) + 1e-06)


def cross(left, right):
    return lax.dot_general(
        left, right, (((1,), (1,)), ((), ())), preferred_element_type=jnp.float32
    )


def linear(y, x, z, core):
    return ((y * 4 + x) * 16 + z) * 2 + core


def spread(flip):
    pairs = []
    for y in range(4):
        for x in range(4):
            for z in range(16):
                for core in range(2):
                    zl, to = 2 * y + x // 2, x % 2
                    target = linear((y + z // 4) % 4, (x + z % 4) % 4, (core ^ flip) * 8 + zl, to)
                    pairs.append((linear(y, x, z, core), target))
    return pairs


def plane_groups():
    groups = []
    for z in range(16):
        for core in range(2):
            zl = z % 8
            y, x = zl // 2, 2 * (zl % 2) + core
            groups.append([linear((y + s // 4) % 4, (x + s % 4) % 4, z, core) for s in range(16)])
    return groups


def body(grads):
    depth = grads.shape[1]
    zh, zl = lax.axis_index("zh"), lax.axis_index("zl")
    first = lax.ppermute(grads, AXES, spread(0))
    second = lax.ppermute(grads, AXES, spread(1))
    mine = jnp.where(zh == 0, jnp.concatenate([first, second]), jnp.concatenate([second, first]))
    columns = lax.all_gather(mine, AXES, axis_index_groups=plane_groups(), axis=0, tiled=True)

    rows = grads[None]
    for step in (4, 2, 1):
        other = lax.ppermute(rows, Z, [(z, z ^ step) for z in range(16)])
        rows = jnp.stack([rows, other], axis=1 if step != 4 else 0).reshape(-1, *grads.shape)
    rows = rows.reshape(8, 8, depth)
    other = lax.ppermute(rows, "core", [(0, 1), (1, 0)])
    both = jnp.stack([rows, other]).reshape(128, depth)
    left = inverse_norms(both)
    right = inverse_norms(columns)
    gram = left[:, None] * cross(both, columns) * right[None, :]
    gram = gram.reshape(2, 2, 2, 2, 8, 256)
    core = lax.axis_index("core")
    gram = jnp.where(core == 1, gram[::-1], gram)
    gram = jnp.where((zl >> 2) & 1 == 1, gram[:, ::-1], gram)
    gram = jnp.where((zl >> 1) & 1 == 1, gram[:, :, ::-1], gram)
    gram = jnp.where(zl & 1 == 1, gram[:, :, :, ::-1], gram)
    return gram.transpose(1, 2, 3, 0, 4, 5).reshape(128, 256)


def solution(mesh):
    fine = Mesh(mesh.devices.reshape(SIZES), AXES)
    return jax.shard_map(
        body, mesh=fine, in_specs=(P(AXES, None),), out_specs=P(("y", "x", "zh"), ("zl", "core")), check_vma=False
    )
```

```python
import jax
import jax.numpy as jnp
from jax import lax
from jax.sharding import Mesh, PartitionSpec as P

AXES = ("y", "x", "zh", "zl", "core")
SIZES = (4, 4, 2, 8, 2)
Z = ("zh", "zl")
YZ = ("y", "zh", "zl", "core")


def squares(block):
    wide = block.astype(jnp.float32)
    return jnp.sum(wide * wide, axis=-1)


def cross(left, right):
    return lax.dot_general(
        left, right, (((1,), (1,)), ((), ())), preferred_element_type=jnp.float32
    )


def spread(half, away):
    pairs = []
    for y in range(4):
        for z in range(16):
            for core in range(2):
                m, zh = z % 2 ^ half, z // 8 ^ away
                target_y = y ^ (z // 2 % 4)
                pairs.append((((y * 16 + z) * 2) + core, ((target_y * 16 + zh * 8 + 2 * y + m) * 2) + core))
    return pairs


def swap(flag, array, axis):
    return jnp.where(flag == 1, jnp.flip(array, axis), array)


def body(grads):
    count, depth = grads.shape
    part = depth // 4
    zh, zl, core = (lax.axis_index(a) for a in ("zh", "zl", "core"))

    held = lax.all_to_all(grads.reshape(count, 4, part).transpose(1, 0, 2), "x", 0, 0, tiled=True)

    odd = zl % 2 == 1
    near = jnp.where(odd, held[2:], held[:2])
    far = jnp.where(odd, held[:2], held[2:])
    sent = [lax.ppermute(near if half == 0 else far, YZ, spread(half, away)) for half in (0, 1) for away in (0, 1)]
    mine = jnp.stack(sent)
    columns = lax.all_to_all(jnp.broadcast_to(mine[None], (4, *mine.shape)), "y", 0, 0, tiled=True)
    columns = columns.reshape(16, 2, count, part)
    own = jnp.where(core == 0, columns[:, 0], columns[:, 1])
    give = jnp.where(core == 0, columns[:, 1], columns[:, 0])
    columns = jnp.stack([own, lax.ppermute(give, "core", [(0, 1), (1, 0)])])
    columns = columns.reshape(32 * count, part)

    rows = held[:, None]
    for step in (4, 2, 1):
        other = lax.ppermute(rows, Z, [(z, z ^ step) for z in range(16)])
        rows = jnp.stack([rows, other], axis=2).reshape(4, -1, count, part)
    other = lax.ppermute(rows, "core", [(0, 1), (1, 0)])
    rows = jnp.stack([rows, other], axis=1).reshape(4, 16 * count, part)

    products = cross(rows.reshape(-1, part), columns).reshape(4, 16 * count, 32 * count)
    extra = jnp.zeros((4, 8, 32 * count), jnp.float32)
    extra = extra.at[:, 0, : 16 * count].set(squares(rows))
    extra = extra.at[:, 1].set(squares(columns)[None])
    message = jnp.concatenate([products, extra], axis=1)
    total = jnp.sum(lax.all_to_all(message, "x", 0, 0, tiled=True).reshape(4, -1, 32 * count), axis=0)
    left = lax.rsqrt(total[16 * count, : 16 * count] + 1e-06)
    right = lax.rsqrt(total[16 * count + 1] + 1e-06)
    gram = left[:, None] * total[: 16 * count] * right[None, :]

    gram = gram.reshape(2, 2, 2, 2, count, 32 * count)
    gram = swap(core, gram, 0)
    for axis, bit in ((1, 2), (2, 1), (3, 0)):
        gram = swap(zl >> bit & 1, gram, axis)
    gram = gram.transpose(1, 2, 3, 0, 4, 5).reshape(16 * count, 32 * count).T
    gram = gram.reshape(2, 2, 2, 2, 2, count, 16 * count)
    for axis, flag in ((0, core), (1, zl >> 2 & 1), (2, zl >> 1 & 1), (3, zl & 1), (4, zh)):
        gram = swap(flag, gram, axis)
    gram = gram.transpose(4, 1, 2, 3, 0, 5, 6).reshape(32 * count, 16 * count)
    return gram.T


def solution(mesh):
    fine = Mesh(mesh.devices.reshape(SIZES), AXES)
    return jax.shard_map(
        body, mesh=fine, in_specs=(P(AXES, None),), out_specs=P(("y", "x", "zh"), ("zl", "core")), check_vma=False
    )
```

```python
import jax
import jax.numpy as jnp
from jax import lax
from jax.sharding import Mesh, PartitionSpec as P

AXES = ("y", "x", "zh", "za", "zb", "core")
SIZES = (4, 4, 2, 4, 2, 2)
SUM = ("y", "zb")


def squares(block):
    wide = block.astype(jnp.float32)
    return jnp.sum(wide * wide, axis=-1)


def cross(left, right):
    return lax.dot_general(
        left, right, (((1,), (1,)), ((), ())), preferred_element_type=jnp.float32
    )


def swap(flag, array, axis):
    return jnp.where(flag == 1, jnp.flip(array, axis), array)


def to_all(array, axes, size):
    return lax.all_to_all(jnp.broadcast_to(array[None], (size, *array.shape)), axes, 0, 0)


def body(grads):
    count, depth = grads.shape
    part = depth // 8
    za = lax.axis_index("za")

    held = lax.all_to_all(grads.reshape(count, 8, part).transpose(1, 0, 2), SUM, 0, 0)
    held = held.reshape(4, 2 * count, part)

    columns = lax.all_to_all(jnp.concatenate([held, held]), ("zh", "za"), 0, 0)
    columns = to_all(columns, "x", 4).reshape(2, 2, 16, count, part)
    columns = lax.all_to_all(columns.swapaxes(0, 1), "core", 0, 0)
    columns = columns.transpose(1, 2, 0, 3, 4).reshape(2, 32 * count, part)

    rows = held[:, None]
    for step in (2, 1):
        other = lax.ppermute(rows, "za", [(z, z ^ step) for z in range(4)])
        rows = jnp.stack([rows, other], axis=2).reshape(4, -1, 2 * count, part)
    rows = to_all(rows, "core", 2)
    rows = rows.swapaxes(0, 1).reshape(4, 16 * count, part)

    products = cross(rows.reshape(64 * count, part), columns.reshape(64 * count, part))
    products = products.reshape(4, 16 * count, 2, 32 * count).swapaxes(1, 2)
    extra = jnp.zeros((4, 2, 8, 32 * count), jnp.float32)
    extra = extra.at[:, :, 0, : 16 * count].set(squares(rows)[:, None])
    extra = extra.at[:, :, 1].set(squares(columns)[None])
    message = jnp.concatenate([products, extra], axis=2).reshape(8, -1, 32 * count)
    total = jnp.sum(lax.all_to_all(message, SUM, 0, 0), axis=0)
    left = lax.rsqrt(total[16 * count, : 16 * count] + 1e-06)
    right = lax.rsqrt(total[16 * count + 1] + 1e-06)
    gram = left[:, None] * total[: 16 * count] * right[None, :]

    gram = gram.reshape(2, 2, 2, 2, count, 32 * count)
    gram = swap(za >> 1, gram, 1)
    gram = swap(za & 1, gram, 2)
    return gram.transpose(1, 2, 3, 0, 4, 5).reshape(16 * count, 32 * count)


def solution(mesh):
    fine = Mesh(mesh.devices.reshape(SIZES), AXES)
    return jax.shard_map(
        body,
        mesh=fine,
        in_specs=(P(AXES, None),),
        out_specs=P(("y", "x", "zh"), ("za", "zb", "core")),
        check_vma=False,
    )
```

```python
import jax
import jax.numpy as jnp
from jax import lax
from jax.sharding import Mesh, PartitionSpec as P

AXES = ("y", "x", "zh", "zl", "core")
SIZES = (4, 4, 2, 8, 2)
Z = ("zh", "zl")


def squares(block):
    wide = block.astype(jnp.float32)
    return jnp.sum(wide * wide, axis=-1)


def cross(left, right):
    return lax.dot_general(
        left, right, (((1,), (1,)), ((), ())), preferred_element_type=jnp.float32
    )


def linear(y, x, z, core):
    return ((y * 4 + x) * 16 + z) * 2 + core


def spread(flip):
    pairs = []
    for y in range(4):
        for x in range(4):
            for z in range(16):
                for core in range(2):
                    plane = (core ^ flip) * 8 + 2 * y + x // 2
                    pairs.append((linear(y, x, z, core), linear(y ^ z // 4, x ^ z % 4, plane, x % 2)))
    return pairs


def swap(flag, array, axis):
    return jnp.where(flag == 1, jnp.flip(array, axis), array)


def to_all(array, axes):
    return lax.all_to_all(jnp.broadcast_to(array[None], (4, *array.shape)), axes, 0, 0)


def body(grads):
    count, depth = grads.shape
    half = depth // 2
    zh, zl, core = (lax.axis_index(a) for a in ("zh", "zl", "core"))

    first = lax.ppermute(grads, AXES, spread(0))
    second = lax.ppermute(grads, AXES, spread(1))
    mine = jnp.where(zh == 0, jnp.concatenate([first, second]), jnp.concatenate([second, first]))
    low = to_all(to_all(mine[:, :half], "y"), "x")
    high = to_all(to_all(mine[:, half:], "x"), "y")

    rows = grads[None]
    for step in (4, 2, 1):
        other = lax.ppermute(rows, Z, [(z, z ^ step) for z in range(16)])
        rows = jnp.stack([rows, other], axis=1 if step != 4 else 0).reshape(-1, *grads.shape)
    rows = rows.reshape(8 * count, depth)
    other = lax.ppermute(rows, "core", [(0, 1), (1, 0)])
    rows = jnp.concatenate([rows, other])

    size = 2 * count
    low_part = cross(low.reshape(16 * size, half), rows[:, :half]).reshape(4, 4, size, -1)
    high_part = cross(high.reshape(16 * size, half), rows[:, half:]).reshape(4, 4, size, -1)
    gram = low_part.swapaxes(0, 1) + high_part
    right = lax.rsqrt(squares(low).swapaxes(0, 1) + squares(high) + 1e-06)
    left = lax.rsqrt(squares(rows) + 1e-06)
    gram = gram * right[..., None] * left
    gram = gram.reshape(2, 2, 2, 2, size, -1)
    for axis, flag in ((0, zl >> 2 & 1), (1, zl >> 1 & 1), (2, zl & 1), (3, core)):
        gram = swap(flag, gram, axis)
    gram = gram.reshape(16 * size, -1).T.reshape(2, 2, 2, 2, count, -1)
    for axis, flag in ((0, core), (1, zl >> 2 & 1), (2, zl >> 1 & 1), (3, zl & 1)):
        gram = swap(flag, gram, axis)
    return gram.transpose(1, 2, 3, 0, 4, 5).reshape(16 * count, -1)


def solution(mesh):
    fine = Mesh(mesh.devices.reshape(SIZES), AXES)
    return jax.shard_map(
        body, mesh=fine, in_specs=(P(AXES, None),), out_specs=P(("y", "x", "zh"), ("zl", "core")), check_vma=False
    )
```

```python
import jax
import jax.numpy as jnp
from jax import lax
from jax.sharding import Mesh, PartitionSpec as P

AXES = ("y", "xh", "xl", "zh", "zl", "core")
SIZES = (4, 2, 2, 2, 8, 2)
PLANE = ("y", "xh")
Z = ("zh", "zl")
TRADE = [(0, 1), (1, 0)]


def squares(block):
    wide = block.astype(jnp.float32)
    return jnp.sum(wide * wide, axis=-1)


def cross(left, right):
    return lax.dot_general(
        left, right, (((1,), (1,)), ((), ())), preferred_element_type=jnp.float32
    )


def linear(plane, xl, z, core):
    return ((plane * 2 + xl) * 16 + z) * 2 + core


def spread(part, away):
    pairs = []
    for plane in range(8):
        for xl in range(2):
            for zh in range(2):
                for zl in range(8):
                    for core in range(2):
                        target = linear(plane ^ zl, zh ^ part, (core ^ away) * 8 + plane, xl)
                        pairs.append((linear(plane, xl, zh * 8 + zl, core), target))
    return pairs


def swap(flag, array, axis):
    return jnp.where(flag == 1, jnp.flip(array, axis), array)


def body(grads):
    count, depth = grads.shape
    half = depth // 2
    zh, zl, core, xl = (lax.axis_index(a) for a in ("zh", "zl", "core", "xl"))
    low, high = grads[:, :half], grads[:, half:]

    near, far = jnp.where(zh == 0, low, high), jnp.where(zh == 0, high, low)
    sent = [lax.ppermute((near, far)[part], AXES, spread(part, away)) for part in (0, 1) for away in (0, 1)]
    mine = jnp.stack(sent)
    columns = lax.all_to_all(jnp.broadcast_to(mine[None], (8, *mine.shape)), PLANE, 0, 0)
    columns = columns.reshape(32 * count, half)

    keep, give = jnp.where(xl == 0, low, high), jnp.where(xl == 0, high, low)
    rows = jnp.stack([keep, lax.ppermute(give, "xl", TRADE)])[:, None]
    for step in (4, 2, 1):
        other = lax.ppermute(rows, Z, [(z, z ^ step) for z in range(16)])
        rows = jnp.stack([rows, other], axis=2).reshape(2, -1, count, half)
    other = lax.ppermute(rows, "core", TRADE)
    rows = jnp.stack([rows, other], axis=1).reshape(2, 16 * count, half)

    lengths = squares(columns)
    trade = lambda array: jnp.flip(array.reshape(8, 2, 2 * count, -1), 1).reshape(array.shape)
    extra = jnp.zeros((2, 8, 16 * count), jnp.float32)
    extra = extra.at[:, 0].set(squares(rows)).at[0, 1:3].set(lengths.reshape(2, -1))
    extra = extra.at[1, 1:3].set(trade(lengths[:, None]).reshape(2, -1))
    own = jnp.concatenate([cross(columns, rows[0]), extra[0]])
    other = jnp.concatenate([trade(cross(columns, rows[1])), extra[1]])
    total = own + lax.ppermute(other, "xl", TRADE)
    gram, extra = total[: 32 * count], lax.rsqrt(total[32 * count :] + 1e-06)
    gram = gram * extra[1:3].reshape(-1)[:, None] * extra[0]

    gram = gram.reshape(2, 2, 2, 2, 2, count, -1)
    for axis, flag in ((0, zl >> 2 & 1), (1, zl >> 1 & 1), (2, zl & 1), (3, xl), (4, zh)):
        gram = swap(flag, gram, axis)
    gram = gram.transpose(3, 0, 1, 2, 4, 5, 6).reshape(32 * count, -1).T.reshape(2, 2, 2, 2, count, -1)
    for axis, flag in ((0, core), (1, zl >> 2 & 1), (2, zl >> 1 & 1), (3, zl & 1)):
        gram = swap(flag, gram, axis)
    return gram.transpose(1, 2, 3, 0, 4, 5).reshape(16 * count, -1)


def solution(mesh):
    fine = Mesh(mesh.devices.reshape(SIZES), AXES)
    return jax.shard_map(
        body, mesh=fine, in_specs=(P(AXES, None),), out_specs=P(("y", "xh", "xl", "zh"), ("zl", "core")), check_vma=False
    )
```

```python
import jax
import jax.numpy as jnp
from jax import lax
from jax.sharding import Mesh, PartitionSpec as P

AXES = ("y", "x", "zh", "za", "zb", "core")
SIZES = (4, 4, 2, 4, 2, 2)
SUM = ("y", "zb")


def squares(block):
    wide = block.astype(jnp.float32)
    return jnp.sum(wide * wide, axis=-1)


def cross(left, right):
    return lax.dot_general(
        left, right, (((1,), (1,)), ((), ())), preferred_element_type=jnp.float32
    )


def swap(flag, array, axis):
    return jnp.where(flag == 1, jnp.flip(array, axis), array)


def to_all(array, axes, size):
    return lax.all_to_all(jnp.broadcast_to(array[None], (size, *array.shape)), axes, 0, 0)


def body(grads):
    count, depth = grads.shape
    part = depth // 8
    za = lax.axis_index("za")

    held = lax.all_to_all(grads.reshape(count, 8, part).transpose(1, 0, 2), SUM, 0, 0)
    held = held.reshape(4, 2 * count, part)

    columns = lax.all_to_all(jnp.concatenate([held, held]), ("zh", "za"), 0, 0)
    columns = to_all(columns, "x", 4).reshape(2, 2, 16, count, part)
    core = lax.axis_index("core")
    keep = jnp.where(core == 0, columns[:, 0], columns[:, 1])
    give = jnp.where(core == 0, columns[:, 1], columns[:, 0])
    give = lax.ppermute(give, "core", [(0, 1), (1, 0)])
    columns = jnp.where(core == 0, jnp.stack([keep, give], 2), jnp.stack([give, keep], 2))
    columns = columns.reshape(2, 32 * count, part)

    rows = held[:, None]
    for step in (2, 1):
        other = lax.ppermute(rows, "za", [(z, z ^ step) for z in range(4)])
        rows = jnp.stack([rows, other], axis=2).reshape(4, -1, 2 * count, part)
    other = lax.ppermute(rows, "core", [(0, 1), (1, 0)])
    rows = jnp.stack([rows, other], axis=1).reshape(4, 16 * count, part)

    products = cross(rows.reshape(64 * count, part), columns.reshape(64 * count, part))
    products = products.reshape(4, 16 * count, 2, 32 * count).swapaxes(1, 2)
    extra = jnp.zeros((4, 2, 8, 32 * count), jnp.float32)
    extra = extra.at[:, :, 0, : 16 * count].set(squares(rows)[:, None])
    extra = extra.at[:, :, 1].set(squares(columns)[None])
    message = jnp.concatenate([products, extra], axis=2).reshape(8, -1, 32 * count)
    total = jnp.sum(lax.all_to_all(message, SUM, 0, 0), axis=0)
    left = lax.rsqrt(total[16 * count, : 16 * count] + 1e-06)
    right = lax.rsqrt(total[16 * count + 1] + 1e-06)
    gram = left[:, None] * total[: 16 * count] * right[None, :]

    gram = gram.reshape(2, 2, 2, 2, count, 32 * count)
    gram = swap(lax.axis_index("core"), gram, 0)
    gram = swap(za >> 1, gram, 1)
    gram = swap(za & 1, gram, 2)
    return gram.transpose(1, 2, 3, 0, 4, 5).reshape(16 * count, 32 * count)


def solution(mesh):
    fine = Mesh(mesh.devices.reshape(SIZES), AXES)
    return jax.shard_map(
        body,
        mesh=fine,
        in_specs=(P(AXES, None),),
        out_specs=P(("y", "x", "zh"), ("za", "zb", "core")),
        check_vma=False,
    )
```

```python
import jax
import jax.numpy as jnp
from jax import lax
from jax.sharding import Mesh, PartitionSpec as P

AXES = ("y", "xh", "xl", "zh", "za", "zb", "core")
SIZES = (4, 2, 2, 2, 4, 2, 2)
SUM = ("y", "zb")
TRADE = [(0, 1), (1, 0)]


def squares(block):
    wide = block.astype(jnp.float32)
    return jnp.sum(wide * wide, axis=-1)


def cross(left, right):
    return lax.dot_general(
        left, right, (((1,), (1,)), ((), ())), preferred_element_type=jnp.float32
    )


def swap(flag, array, axis):
    return jnp.where(flag == 1, jnp.flip(array, axis), array)


def body(grads):
    count, depth = grads.shape
    part = depth // 8
    za, core = (lax.axis_index(a) for a in ("za", "core"))

    held = lax.all_to_all(grads.reshape(count, 8, part).transpose(1, 0, 2), SUM, 0, 0)
    held = held.reshape(4, 2 * count, part)

    columns = lax.all_to_all(jnp.concatenate([held, held]), ("zh", "za"), 0, 0)
    columns = columns.reshape(16 * count, part)
    columns = lax.all_to_all(jnp.broadcast_to(columns[None], (4, *columns.shape)), ("xh", "xl"), 0, 0)
    columns = columns.reshape(2, 2, 16 * count, part)
    own = lax.dynamic_index_in_dim(columns, core, 1, keepdims=False)
    other = lax.ppermute(lax.dynamic_index_in_dim(columns, 1 - core, 1, keepdims=False), "core", TRADE)
    blocks = [block.reshape(32 * count, part) for block in (own, other)]

    rows = held[:, None]
    for step in (2, 1):
        other = lax.ppermute(rows, "za", [(z, z ^ step) for z in range(4)])
        rows = jnp.stack([rows, other], axis=2).reshape(4, -1, 2 * count, part)
    other = lax.ppermute(rows, "core", TRADE)
    rows = jnp.stack([rows, other], axis=1).reshape(4, 16 * count, part)

    lines = rows.reshape(64 * count, part)
    products = jnp.stack([cross(block, lines).reshape(2, 16 * count, 4, -1) for block in blocks], axis=1)
    products = products.reshape(2, 32 * count, 4, -1).transpose(2, 0, 1, 3)
    wide = jnp.stack([squares(block).reshape(2, -1) for block in blocks], axis=1)
    extra = jnp.zeros((4, 2, 8, 16 * count), jnp.float32)
    extra = extra.at[:, :, 0].set(squares(rows)[:, None])
    extra = extra.at[:, :, 1:3].set(wide[None])
    message = jnp.concatenate([products, extra], axis=2)
    total = jnp.sum(lax.all_to_all(message.reshape(8, -1, 16 * count), SUM, 0, 0), axis=0)
    gram, extra = total[: 32 * count], lax.rsqrt(total[32 * count :] + 1e-06)
    gram = gram * extra[1:3].reshape(-1)[:, None] * extra[0]

    gram = swap(core, gram.reshape(2, 16, count, -1), 0).swapaxes(0, 1)
    gram = gram.reshape(32 * count, -1).T.reshape(2, 2, 2, 2, count, -1)
    for axis, flag in ((0, core), (1, za >> 1), (2, za & 1)):
        gram = swap(flag, gram, axis)
    return gram.transpose(1, 2, 3, 0, 4, 5).reshape(16 * count, -1)


def solution(mesh):
    fine = Mesh(mesh.devices.reshape(SIZES), AXES)
    return jax.shard_map(
        body,
        mesh=fine,
        in_specs=(P(AXES, None),),
        out_specs=P(("y", "xh", "xl", "zh"), ("za", "zb", "core")),
        check_vma=False,
    )
```

```python
import jax
import jax.numpy as jnp
from jax import lax
from jax.sharding import Mesh, PartitionSpec as P

AXES = ("y", "xh", "xl", "zh", "za", "zb", "core")
SIZES = (4, 2, 2, 2, 4, 2, 2)
SUM = ("y", "zb")
TRADE = [(0, 1), (1, 0)]


def squares(block):
    wide = block.astype(jnp.float32)
    return jnp.sum(wide * wide, axis=-1)


def cross(left, right):
    return lax.dot_general(
        left, right, (((1,), (1,)), ((), ())), preferred_element_type=jnp.float32
    )


def swap(flag, array, axis):
    return jnp.where(flag == 1, jnp.flip(array, axis), array)


def body(grads):
    count, depth = grads.shape
    part = depth // 8
    za, core = (lax.axis_index(a) for a in ("za", "core"))

    held = lax.all_to_all(grads.reshape(count, 8, part).transpose(1, 0, 2), SUM, 0, 0)
    held = held.reshape(4, 2 * count, part)

    columns = lax.all_to_all(jnp.concatenate([held, held]), ("zh", "za"), 0, 0)
    columns = columns.reshape(16 * count, part)
    columns = lax.all_to_all(jnp.broadcast_to(columns[None], (4, *columns.shape)), ("xh", "xl"), 0, 0)
    columns = columns.reshape(2, 2, 16 * count, part)
    rows = held[:, None]
    for step in (2, 1):
        other = lax.ppermute(rows, "za", [(z, z ^ step) for z in range(4)])
        rows = jnp.stack([rows, other], axis=2).reshape(4, -1, 2 * count, part)
    columns, rows = lax.optimization_barrier((columns, rows))
    own = lax.dynamic_index_in_dim(columns, core, 1, keepdims=False)
    other = lax.ppermute(lax.dynamic_index_in_dim(columns, 1 - core, 1, keepdims=False), "core", TRADE)
    blocks = [block.reshape(32 * count, part) for block in (own, other)]
    other = lax.ppermute(rows, "core", TRADE)
    rows = jnp.stack([rows, other], axis=1).reshape(4, 16 * count, part)

    lines = rows.reshape(64 * count, part)
    products = jnp.stack([cross(block, lines).reshape(2, 16 * count, 4, -1) for block in blocks], axis=1)
    products = products.reshape(2, 32 * count, 4, -1).transpose(2, 0, 1, 3)
    wide = jnp.stack([squares(block).reshape(2, -1) for block in blocks], axis=1)
    extra = jnp.zeros((4, 2, 8, 16 * count), jnp.float32)
    extra = extra.at[:, :, 0].set(squares(rows)[:, None])
    extra = extra.at[:, :, 1:3].set(wide[None])
    message = jnp.concatenate([products, extra], axis=2)
    total = jnp.sum(lax.all_to_all(message.reshape(8, -1, 16 * count), SUM, 0, 0), axis=0)
    gram, extra = total[: 32 * count], lax.rsqrt(total[32 * count :] + 1e-06)
    gram = gram * extra[1:3].reshape(-1)[:, None] * extra[0]

    gram = swap(core, gram.reshape(2, 16, count, -1), 0).swapaxes(0, 1)
    gram = gram.reshape(32 * count, -1).T.reshape(2, 2, 2, 2, count, -1)
    for axis, flag in ((0, core), (1, za >> 1), (2, za & 1)):
        gram = swap(flag, gram, axis)
    return gram.transpose(1, 2, 3, 0, 4, 5).reshape(16 * count, -1)


def solution(mesh):
    fine = Mesh(mesh.devices.reshape(SIZES), AXES)
    return jax.shard_map(
        body,
        mesh=fine,
        in_specs=(P(AXES, None),),
        out_specs=P(("y", "xh", "xl", "zh"), ("za", "zb", "core")),
        check_vma=False,
    )
```

```python
import jax
import jax.numpy as jnp
from jax import lax
from jax.sharding import Mesh, PartitionSpec as P

AXES = ("y", "xh", "xl", "zh", "za", "zb", "core")
SIZES = (4, 2, 2, 2, 4, 2, 2)
SUM = ("y", "zb")
TRADE = [(0, 1), (1, 0)]


def squares(block):
    wide = block.astype(jnp.float32)
    return jnp.sum(wide * wide, axis=-1)


def cross(left, right):
    return lax.dot_general(
        left, right, (((1,), (1,)), ((), ())), preferred_element_type=jnp.float32
    )


def swap(flag, array, axis):
    return jnp.where(flag == 1, jnp.flip(array, axis), array)


def body(grads):
    count, depth = grads.shape
    part = depth // 8
    za, core = (lax.axis_index(a) for a in ("za", "core"))

    held = lax.all_to_all(grads.reshape(count, 8, part).transpose(1, 0, 2), SUM, 0, 0)
    held = held.reshape(4, 2 * count, part)

    columns = lax.all_to_all(jnp.concatenate([held, held]), ("zh", "za"), 0, 0)
    columns = columns.reshape(16 * count, part)
    columns = lax.all_to_all(jnp.broadcast_to(columns[None], (4, *columns.shape)), ("xh", "xl"), 0, 0)
    columns = columns.reshape(2, 2, 16 * count, part)
    own = lax.dynamic_index_in_dim(columns, core, 1, keepdims=False)
    other = lax.ppermute(lax.dynamic_index_in_dim(columns, 1 - core, 1, keepdims=False), "core", TRADE)
    blocks = [block.reshape(32 * count, part) for block in (own, other)]

    rows = held[:, None]
    for step in (2, 1):
        other = lax.ppermute(rows, "za", [(z, z ^ step) for z in range(4)])
        rows = jnp.stack([rows, other], axis=2).reshape(4, -1, 2 * count, part)
    other = lax.ppermute(rows, "core", TRADE)
    rows = jnp.stack([rows, other], axis=1).reshape(4, 16 * count, part)

    lines = rows.reshape(64 * count, part)
    products = jnp.stack([cross(block, lines).reshape(2, 16 * count, 4, -1) for block in blocks], axis=1)
    products = products.reshape(2, 32 * count, 4, -1).swapaxes(1, 2)
    wide = jnp.stack([squares(block).reshape(2, -1) for block in blocks], axis=1)
    extra = jnp.zeros((2, 4, 8, 16 * count), jnp.float32)
    extra = extra.at[:, :, 0].set(squares(rows)[None])
    extra = extra.at[:, :, 1:3].set(wide[:, None])
    message = jnp.concatenate([products, extra], axis=2)
    total = jnp.sum(lax.all_to_all(message.reshape(8, -1, 16 * count), ("zb", "y"), 0, 0), axis=0)
    gram, extra = total[: 32 * count], lax.rsqrt(total[32 * count :] + 1e-06)
    gram = gram * extra[1:3].reshape(-1)[:, None] * extra[0]

    gram = swap(core, gram.reshape(2, 16, count, -1), 0).swapaxes(0, 1)
    gram = gram.reshape(32 * count, -1).T.reshape(2, 2, 2, 2, count, -1)
    for axis, flag in ((0, core), (1, za >> 1), (2, za & 1)):
        gram = swap(flag, gram, axis)
    return gram.transpose(1, 2, 3, 0, 4, 5).reshape(16 * count, -1)


def solution(mesh):
    fine = Mesh(mesh.devices.reshape(SIZES), AXES)
    return jax.shard_map(
        body,
        mesh=fine,
        in_specs=(P(AXES, None),),
        out_specs=P(("y", "xh", "xl", "zh"), ("za", "zb", "core")),
        check_vma=False,
    )
```
